256 devices in a mesh: seq: 64 (over y, z, core), tp: 4 (over x).
Axes of the slice: x: 4, y: 4, z: 8, core: 2. Of those that a mesh axis runs over, the one named last changes fastest.
Arguments:
- tokens: bfloat16 [131072, 4096], P('seq', 'tp'), may hold values from -6 to 6
- norm_gain: bfloat16 [4096], replicated, may hold values from 0.25 to 1.75
- router_weight: bfloat16 [4096], replicated, may hold values from -0.09375 to 0.09375
- w_query: bfloat16 [4096, 2048], P(None, 'tp'), may hold values from -1 to 1
- w_key: bfloat16 [4096, 512], P(None, 'tp'), may hold values from -1 to 1
- w_value: bfloat16 [4096, 512], P(None, 'tp'), may hold values from -0.1875 to 0.1875
- w_out: bfloat16 [2048, 4096], P('tp', 'seq'), may hold values from -0.125 to 0.125
- seg_ids: int32 [32], replicated, may hold values from 0 to 63, as said below
- blk_ids: int32 [32, 2], replicated, may hold values from 0 to 15, as said below
Outputs:
- updated: bfloat16 [128, 128, 4096], P('seq', None, 'tp')
The draws below stay inside these ranges and needn't reach their ends.
Inputs may be any that keep to these rules, and one draw needn't show every extreme that they name: `seg_ids`: Distinct, in increasing order; in every draw all 1 segments of one index of seq are selected, so that one index holds 2 selected blocks. `blk_ids`: each row holds distinct numbers in increasing order.
All inputs are finite; a program needn't handle non-finite values.
Results may differ from the reference program's by a relative error of at most 0.0095.
Values may be sent and summed in bfloat16 or wider, within the bound.
A program may use at most 128 MiB of HBM per device.

```python
import jax
import jax.numpy as jnp
from jax import lax

D = 4096
HEADS = 16
KV_HEADS = 4
HD = 128
BLK = 128
SEG_BLK = 16
PER_SEG = 2
SEG_DEV = 1
NSEG = 64
NSEL_SEG = 32
SEL = 64
TOKENS = 131072
N_SEQ = 64


score_spread = 1.6


def drawn_weight(folded, columns):
    values = jnp.clip(jax.random.normal(folded, (D, columns), jnp.float32), -4.0, 4.0)
    return values * (score_spread / jnp.sqrt(jnp.float32(D)))


def draw_w_query(key, part):
    folded = jax.random.fold_in(key, 21)
    return drawn_weight(folded, HEADS * HD).astype(jnp.bfloat16)


def draw_w_key(key, part):
    folded = jax.random.fold_in(key, 22)
    return drawn_weight(folded, KV_HEADS * HD).astype(jnp.bfloat16)


def draw_seg_ids(key, part):
    key = jax.random.fold_in(key, 11)
    first_key, second_key = jax.random.split(key)
    chosen_home = jax.random.randint(first_key, (), 0, N_SEQ)
    order = jax.random.permutation(second_key, NSEG).astype(jnp.int32)
    numbers = jnp.arange(NSEG, dtype=jnp.int32)
    forced = (numbers // SEG_DEV == chosen_home) | (numbers == 0) | (numbers == NSEG - 1)
    scores = jnp.where(forced, -1 - numbers, order)
    unused, picked = lax.top_k(-scores, NSEL_SEG)
    return jnp.sort(picked).astype(jnp.int32)


def draw_blk_ids(key, part):
    key = jax.random.fold_in(key, 12)
    raw = jax.random.randint(key, (NSEL_SEG, SEG_BLK), 0, 1 << 20)
    scores = raw * SEG_BLK + jnp.arange(SEG_BLK, dtype=jnp.int32)[None, :]
    scores = scores.at[0, 0].set(-1)
    scores = scores.at[NSEL_SEG - 1, SEG_BLK - 1].set(-1)
    order = jnp.argsort(scores, axis=1, stable=True)[:, :PER_SEG]
    return jnp.sort(order, axis=1).astype(jnp.int32)


def steps_of(rng, shape, cuts, low, largest):
    def one(axis_at, parts):
        heights = jax.random.uniform(jax.random.fold_in(jax.random.fold_in(rng, 6), axis_at), (parts,), jnp.float32, low / len(cuts), largest / len(cuts))
        return jnp.repeat(jnp.exp(heights), shape[axis_at] // parts).reshape((-1,) + (1,) * (len(shape) - axis_at - 1))

    gain = one(*cuts[0])
    for cut in cuts[1:]:
        gain = gain * one(*cut)
    return gain


def normal_values(own_key, shape, scale, most, cuts=(), kind=jnp.bfloat16):
    factor_of = steps_of(own_key, shape, cuts, -0.22, 0.18) if cuts else 1.0
    values = jax.random.normal(own_key, shape, jnp.float32) * scale * factor_of
    return jnp.minimum(jnp.maximum(values, -most), most).astype(kind)


def setup_inputs(seed: int = 0) -> dict:
    key_of = jax.random.split(jax.random.key(seed), 10)
    tokens = normal_values(key_of[0], (TOKENS, D), 1.0, 6.0, ((0, 64), (1, 4)))
    norm_gain = jnp.clip(1.0 + 0.15 * jax.random.normal(key_of[1], (D,), jnp.float32), 0.25, 1.75).astype(jnp.bfloat16)
    router_weight = normal_values(key_of[2], (D,), D ** -0.5, 0.09375)
    w_query = draw_w_query(jax.random.fold_in(key_of[9], 71), 0)
    w_key = draw_w_key(jax.random.fold_in(key_of[9], 71), 0)
    w_value = normal_values(key_of[5], (D, KV_HEADS * HD), (D // 4) ** -0.5, 0.1875, ((1, 4),))
    w_out = normal_values(key_of[6], (HEADS * HD, D), (HEADS * HD) ** -0.5, 0.125, ((0, 4), (1, 64)))
    seg_ids = draw_seg_ids(jax.random.fold_in(key_of[9], 71), 0)
    blk_ids = draw_blk_ids(jax.random.fold_in(key_of[9], 71), 0)
    return {"tokens": tokens, "norm_gain": norm_gain, "router_weight": router_weight, "w_query": w_query, "w_key": w_key, "w_value": w_value, "w_out": w_out, "seg_ids": seg_ids, "blk_ids": blk_ids}


def reference(tokens, norm_gain, router_weight, w_query, w_key, w_value, w_out, seg_ids, blk_ids):
    home_blocks = SEG_DEV * SEG_BLK
    slot_count = SEG_DEV * PER_SEG
    blocks = (seg_ids[:, None] * SEG_BLK + blk_ids).reshape(-1).astype(jnp.int32)
    homes = blocks // home_blocks
    ranks = jnp.arange(SEL, dtype=jnp.int32)
    slots = ranks - lax.optimization_barrier(jnp.sum((homes[None, :] < homes[:, None]).astype(jnp.int32), axis=1))
    sel_rows = tokens.reshape(TOKENS // BLK, BLK, D)[blocks].reshape(SEL * BLK, D)
    floats = sel_rows.astype(jnp.float32)
    square_mean = lax.optimization_barrier(jnp.mean(floats * floats, axis=-1, keepdims=True))
    normed = (floats * lax.rsqrt(square_mean + 1e-05) * norm_gain.astype(jnp.float32)).astype(jnp.bfloat16)
    gate = jax.nn.sigmoid(jnp.dot(sel_rows, router_weight, preferred_element_type=jnp.float32))
    queries = jnp.dot(normed, w_query, preferred_element_type=jnp.float32).astype(jnp.bfloat16)
    key_rows = jnp.dot(normed, w_key, preferred_element_type=jnp.float32).astype(jnp.bfloat16)
    value_rows = jnp.dot(normed, w_value, preferred_element_type=jnp.float32).astype(jnp.bfloat16)
    positions = (blocks[:, None] * BLK + jnp.arange(BLK, dtype=jnp.int32)[None, :]).reshape(-1)
    visible = positions[None, :] <= positions[:, None]
    group = HEADS // KV_HEADS

    def one_head(head):
        head = head.astype(jnp.int32)
        query_head = lax.dynamic_slice_in_dim(queries, head * HD, HD, 1)
        key_head = lax.dynamic_slice_in_dim(key_rows, head // group * HD, HD, 1)
        value_head = lax.dynamic_slice_in_dim(value_rows, head // group * HD, HD, 1)
        scores = jnp.dot(query_head, key_head.T, preferred_element_type=jnp.float32) / jnp.sqrt(jnp.float32(HD))
        scores = jnp.where(visible, scores, -jnp.inf)
        weights = jax.nn.softmax(scores, axis=-1).astype(jnp.bfloat16)
        return jnp.dot(weights, value_head, preferred_element_type=jnp.float32).astype(jnp.bfloat16)
    per_head = lax.map(one_head, jnp.arange(HEADS, dtype=jnp.int32))
    heads_out = jnp.transpose(per_head, (1, 0, 2)).reshape(SEL * BLK, HEADS * HD)
    attended = jnp.dot(heads_out, w_out, preferred_element_type=jnp.float32)
    new_rows = (floats + gate[:, None] * attended).astype(jnp.bfloat16).reshape(SEL, BLK, D)
    updated = jnp.zeros((N_SEQ * slot_count, BLK, D), jnp.bfloat16)
    return updated.at[homes * slot_count + slots].set(new_rows)
```

```python
import functools

import jax
import jax.numpy as jnp
from jax import lax
from jax.experimental import pallas as pl
from jax.experimental.pallas import tpu as pltpu
from jax.sharding import PartitionSpec as P

MESH = pl.DeviceIdType.MESH
F32 = jnp.float32
BF16 = jnp.bfloat16

NY, NZ, NX = 4, 8, 4
HD = 128
BLK = 128
LOCAL_HEADS = 4
ROWS = 2 * BLK
QROWS = LOCAL_HEADS * BLK
FEATS = 1024
SEGS = 32
KEY_SEGS = 4
LOG2E = 1.4426950408889634
Q_SCALE = LOG2E / (128.0**0.5)
MASKED = -1e30

Y_FIRST = 96
PY, PZ, RZ, RY, SIB, COPIES = 0, 4, 12, 20, 44, 56


def dot(a, b):
    return jnp.dot(a, b, preferred_element_type=F32)


def dot_t(a, b):
    return lax.dot_general(a, b, (((1,), (1,)), ((), ())), preferred_element_type=F32)


class Place:
    def __init__(self):
        s = lax.axis_index("seq")
        self.x = lax.axis_index("tp")
        self.s = s
        self.y = s // (NZ * 2)
        self.z = (s // 2) % NZ
        self.c = s % 2

    def at(self, x=None, y=None, z=None, c=None):
        x = self.x if x is None else x
        y = self.y if y is None else y
        z = self.z if z is None else z
        c = self.c if c is None else c
        return (y * (NZ * 2) + z * 2 + c, x)


class Copies:
    def __init__(self, send_sems, recv_sems):
        self.ss, self.rs = send_sems, recv_sems
        self.made = {}

    def send(self, src, dst, k, device):
        copy = pltpu.make_async_remote_copy(
            src_ref=src,
            dst_ref=dst,
            send_sem=self.ss.at[k],
            recv_sem=self.rs.at[k],
            device_id=device,
            device_id_type=MESH,
        )
        copy.start()
        self.made[k] = copy

    def recv(self, k):
        self.made[k].wait_recv()

    def drain(self):
        for copy in self.made.values():
            copy.wait_send()
        self.made = {}


def gather_yz(me, both, cp):
    buf, other = both.at[0], both.at[1]
    up_y, down_y = me.at(y=(me.y + 1) % NY), me.at(y=(me.y + 3) % NY)
    up_z, down_z = me.at(z=(me.z + 1) % NZ), me.at(z=(me.z + 7) % NZ)
    sib = me.at(c=1 - me.c)
    half = Y_FIRST // 2
    mid = Y_FIRST + (256 - Y_FIRST) // 2

    def p(dy, lo=0, hi=Y_FIRST):
        return buf.at[dy, 0, lo:hi]

    def col(dz, lo=0, hi=Y_FIRST):
        return buf.at[:, dz, lo:hi]

    def r(dz, dy=0, lo=Y_FIRST, hi=256):
        return buf.at[dy, dz, lo:hi]

    order = (0, 7, 1, 6, 2, 5, 3, 4)

    def row_out(j):
        cp.send(r(order[j]), r(order[j], 3), RY + j, up_y)
        cp.send(r(order[j]), r(order[j], 1), RY + 8 + j, down_y)

    def row_in(j):
        cp.recv(RY + j)
        if j % 2 == 0:
            cp.send(r(order[j], 3), r(order[j], 2), RY + 16 + j, up_y)
        cp.recv(RY + 8 + j)
        if j % 2 == 1:
            cp.send(r(order[j], 1), r(order[j], 2), RY + 16 + j, down_y)

    def sib_col(j, dz):
        cp.send(col(dz), other.at[:, dz, 0:Y_FIRST], SIB + j, sib)

    def sib_row(j, dy):
        cp.send(buf.at[dy, :, Y_FIRST:256], other.at[dy, :, Y_FIRST:256], SIB + 8 + j, sib)

    cp.send(p(0), p(3), PY, up_y)
    cp.send(p(0), p(1), PY + 1, down_y)
    cp.send(r(0), r(7), RZ, up_z)
    cp.send(r(0), r(1), RZ + 1, down_z)
    row_out(0)
    yield
    cp.recv(PY)
    cp.send(p(3, 0, half), p(2, 0, half), PY + 2, up_y)
    cp.recv(PY + 1)
    cp.send(p(1, half, Y_FIRST), p(2, half, Y_FIRST), PY + 3, down_y)
    yield
    cp.recv(RZ)
    cp.send(r(7), r(6), RZ + 2, up_z)
    cp.recv(RZ + 1)
    cp.send(r(1), r(2), RZ + 3, down_z)
    row_out(1)
    row_out(2)
    yield
    cp.recv(PY + 2)
    cp.recv(PY + 3)
    cp.send(col(0), col(7), PZ, up_z)
    cp.send(col(0), col(1), PZ + 1, down_z)
    sib_col(0, 0)
    yield
    cp.recv(RZ + 2)
    cp.send(r(6), r(5), RZ + 4, up_z)
    cp.recv(RZ + 3)
    cp.send(r(2), r(3), RZ + 5, down_z)
    row_out(3)
    row_out(4)
    yield
    row_in(0)
    cp.recv(RZ + 4)
    cp.send(r(5, 0, Y_FIRST, mid), r(4, 0, Y_FIRST, mid), RZ + 6, up_z)
    cp.recv(RZ + 5)
    cp.send(r(3, 0, mid, 256), r(4, 0, mid, 256), RZ + 7, down_z)
    row_out(5)
    row_out(6)
    yield
    cp.recv(PZ)
    cp.send(col(7), col(6), PZ + 2, up_z)
    cp.recv(PZ + 1)
    cp.send(col(1), col(2), PZ + 3, down_z)
    sib_col(1, 7)
    sib_col(2, 1)
    yield
    cp.recv(RZ + 6)
    cp.recv(RZ + 7)
    row_out(7)
    sib_row(0, 0)
    row_in(1)
    row_in(2)
    yield
    cp.recv(PZ + 2)
    cp.send(col(6), col(5), PZ + 4, up_z)
    cp.recv(PZ + 3)
    cp.send(col(2), col(3), PZ + 5, down_z)
    sib_col(3, 6)
    sib_col(4, 2)
    row_in(3)
    row_in(4)
    yield
    cp.recv(PZ + 4)
    cp.send(col(5, 0, half), col(4, 0, half), PZ + 6, up_z)
    cp.recv(PZ + 5)
    cp.send(col(3, half, Y_FIRST), col(4, half, Y_FIRST), PZ + 7, down_z)
    sib_col(5, 5)
    sib_col(6, 3)
    row_in(5)
    yield
    row_in(6)
    row_in(7)
    sib_row(1, 3)
    sib_row(2, 1)
    yield
    cp.recv(PZ + 6)
    cp.recv(PZ + 7)
    sib_col(7, 4)
    for j in range(8):
        cp.recv(RY + 16 + j)
    sib_row(3, 2)
    yield
    for j in range(12):
        cp.recv(SIB + j)
    cp.drain()


def ring_x(me, buf, cp, base):
    mid = BLK // 2
    up, down = me.at(x=(me.x + 1) % NX), me.at(x=(me.x + 3) % NX)
    cp.send(buf.at[0], buf.at[3], base, up)
    cp.send(buf.at[0], buf.at[1], base + 1, down)
    yield
    cp.recv(base)
    cp.send(buf.at[3, 0:mid], buf.at[2, 0:mid], base + 2, up)
    cp.recv(base + 1)
    cp.send(buf.at[1, mid:BLK], buf.at[2, mid:BLK], base + 3, down)
    yield
    cp.recv(base + 2)
    cp.recv(base + 3)


def run(steps, count=None):
    if count is None:
        for _ in steps:
            pass
        return
    for _ in range(count):
        next(steps, None)


def kernel(
    seg_ref,
    blk_ref,
    gain_ref,
    router_ref,
    tok_ref,
    wq_hbm,
    wk_hbm,
    wv_hbm,
    wo_ref,
    out_ref,
    tok,
    wq,
    wk,
    wv,
    wkv,
    xg0,
    xg1,
    normed,
    wsend,
    wrecv,
    wg,
    kv0,
    kv1,
    qx,
    acc,
    top,
    gates,
    hg0,
    hg1,
    att,
    local_sems,
    w_ss,
    w_rs,
    gw_ss,
    gw_rs,
    g0_ss,
    g0_rs,
    g1_ss,
    g1_rs,
    x_ss,
    x_rs,
):
    me = Place()
    x, y, z, c = me.x, me.y, me.z, me.c
    xg, hg = (xg0, xg1), (hg0, hg1)
    tok_copy = pltpu.make_async_copy(tok_ref, tok, local_sems.at[0])
    wk_copy = pltpu.make_async_copy(wk_hbm, wk, local_sems.at[1])
    wv_copy = pltpu.make_async_copy(wv_hbm, wv, local_sems.at[2])
    wq_copy = pltpu.make_async_copy(wq_hbm, wq, local_sems.at[3])
    for copy in (tok_copy, wk_copy, wv_copy, wq_copy):
        copy.start()

    sib = me.at(c=1 - c)
    barrier = pltpu.get_barrier_semaphore()
    neighbours = [
        me.at(x=(x + 1) % NX),
        me.at(x=(x + 3) % NX),
        me.at(y=(y + 1) % NY),
        me.at(y=(y + 3) % NY),
        me.at(z=(z + 1) % NZ),
        me.at(z=(z + 7) % NZ),
        sib,
    ]
    for device in neighbours:
        pl.semaphore_signal(barrier, 1, device_id=device, device_id_type=MESH)

    @pl.when(x != y)
    def _():
        for h in range(2):
            pl.semaphore_signal(
                barrier, 1, device_id=me.at(x=y, y=x, c=h), device_id_type=MESH
            )

    here = lax.broadcasted_iota(jnp.int32, (64, 128), 1)
    there = lax.broadcasted_iota(jnp.int32, (64, 128), 0)
    spread = jnp.where(here == there + 64 * c, 1.0, 0.0).astype(BF16)
    for h in range(2):
        wsend[h] = dot(wo_ref[h * 256 : (h + 1) * 256, :], spread).astype(BF16)

    own = me.s

    def look(j, carry):
        rank, hit, first, second = carry
        seg = seg_ref[j]
        same = seg == own
        return (
            rank + jnp.where(seg < own, 1, 0),
            jnp.where(same, 1, hit),
            jnp.where(same, blk_ref[j, 0], first),
            jnp.where(same, blk_ref[j, 1], second),
        )

    zero = jnp.int32(0)
    rank, filled, first, second = lax.fori_loop(0, SEGS, look, (zero, zero, zero, zero))

    tok_copy.wait()
    for s, block in enumerate((first, second)):
        xg[s][0] = tok[block]

    @pl.when(x != y)
    def _():
        pl.semaphore_wait(barrier, 9)

    @pl.when(x == y)
    def _():
        pl.semaphore_wait(barrier, 7)

    xcp = Copies(x_ss, x_rs)
    x0 = ring_x(me, xg0, xcp, 0)
    x1 = ring_x(me, xg1, xcp, 4)
    run(x0, 1)

    def w_copy(h, slot, device):
        return pltpu.make_async_remote_copy(
            src_ref=wsend.at[h],
            dst_ref=wrecv.at[slot],
            send_sem=w_ss.at[h],
            recv_sem=w_rs.at[slot],
            device_id=device,
            device_id_type=MESH,
        )

    @pl.when(x != y)
    def _():
        for h in range(2):
            w_copy(h, c, me.at(x=y, y=x, c=h)).start()

    @pl.when(x == y)
    def _():
        w_copy(1 - c, c, sib).start()
        wrecv[c] = wsend[c]

    wk_copy.wait()
    wv_copy.wait()
    wkv[:, :, 0:HD] = wk[...]
    wkv[:, :, HD : 2 * HD] = wv[...]

    @pl.when(x != y)
    def _():
        for h in range(2):
            w_copy(h, h, me.at(x=y, y=x, c=h)).wait()

    @pl.when(x == y)
    def _():
        w_copy(1 - c, 1 - c, sib).wait()

    wg[0, 0, 0] = wrecv[0] + wrecv[1]
    gw = gather_yz(me, wg, Copies(gw_ss, gw_rs))
    run(gw, 3)

    run(x0, 1)
    run(x1, 1)
    run(gw, 2)

    feat = [(x + d) % NX for d in range(NX)]

    def norm(s):
        rows = slice(s * BLK, (s + 1) * BLK)
        squares = jnp.zeros((BLK, 1), F32)
        routed = jnp.zeros((BLK, 1), F32)
        for d in range(NX):
            part = xg[s][d].astype(F32)
            squares += jnp.sum(part * part, axis=1, keepdims=True)
            routed += jnp.sum(part * router_ref[feat[d]].astype(F32), axis=1, keepdims=True)
        scale = lax.rsqrt(squares * (1.0 / (NX * FEATS)) + 1e-05)
        gates[rows] = jax.nn.sigmoid(routed)
        for d in range(NX):
            normed[d] = (xg[s][d].astype(F32) * scale * gain_ref[feat[d]].astype(F32)).astype(BF16)

    def through(weight):
        total = dot(normed[0], weight[feat[0]])
        for d in range(1, NX):
            total += dot(normed[d], weight[feat[d]])
        return total.astype(BF16)

    def keys(kv):
        found = through(wkv)
        kv[0, 0, 0] = jnp.concatenate([found[:, 0:HD], found[:, HD : 2 * HD]], axis=0)

    def queries(s):
        found = through(wq).astype(F32) * Q_SCALE
        high = found.astype(BF16)
        low = (found - high.astype(F32)).astype(BF16)
        for h in range(LOCAL_HEADS):
            rows = slice(s * QROWS + h * BLK, s * QROWS + (h + 1) * BLK)
            qx[rows, 0:HD] = high[:, h * HD : (h + 1) * HD]
            qx[rows, HD : 2 * HD] = low[:, h * HD : (h + 1) * HD]

    ones = jnp.ones((BLK, HD), BF16)

    def twice(key):
        return jnp.concatenate([key, key], axis=1)

    run(x0)
    norm(0)
    keys(kv0)
    g0 = gather_yz(me, kv0, Copies(g0_ss, g0_rs))
    run(g0, 1)
    wq_copy.wait()
    queries(0)
    run(g0, 2)
    run(gw, 2)
    run(x1, 1)
    run(g0, 1)
    run(gw, 2)
    run(g0, 1)
    run(gw, 2)
    run(g0, 1)
    run(gw)
    run(x1)
    norm(1)
    keys(kv1)
    g1 = gather_yz(me, kv1, Copies(g1_ss, g1_rs))
    run(g1, 1)
    run(g0, 1)
    queries(1)
    run(g0, 1)
    run(g1, 1)

    def own_blocks():
        own0, own1 = kv0[0, 0, 0], kv1[0, 0, 0]
        key0, value0 = own0[0:BLK], own0[BLK : 2 * BLK]
        key1, value1 = own1[0:BLK], own1[BLK : 2 * BLK]
        row = lax.broadcasted_iota(jnp.int32, (QROWS, BLK), 0) % BLK
        column = lax.broadcasted_iota(jnp.int32, (QROWS, BLK), 1)
        seen = column <= row
        q0, q1 = qx[0:QROWS], qx[QROWS : 2 * QROWS]
        s00 = jnp.where(seen, dot_t(q0, twice(key0)), MASKED)
        most = jnp.max(s00, axis=1, keepdims=True)
        top[0:QROWS] = most
        acc[0:QROWS] = dot(
            jnp.exp2(s00 - most).astype(BF16), jnp.concatenate([value0, ones], axis=1)
        )
        s10 = dot_t(q1, twice(key0))
        s11 = jnp.where(seen, dot_t(q1, twice(key1)), MASKED)
        most = jnp.max(jnp.maximum(s10, s11), axis=1, keepdims=True)
        top[QROWS : 2 * QROWS] = most
        acc[QROWS : 2 * QROWS] = dot(
            jnp.exp2(s10 - most).astype(BF16), jnp.concatenate([value0, ones], axis=1)
        ) + dot(jnp.exp2(s11 - most).astype(BF16), jnp.concatenate([value1, ones], axis=1))

    own_blocks()
    run(g0, 1)
    run(g1, 2)
    run(g0, 1)
    run(g1, 1)
    run(g0, 1)
    run(g1, 1)
    run(g0)

    stand_in = jnp.broadcast_to(kv0[0, 0, 0][0:1], (BLK, HD))
    nothing = jnp.zeros((BLK, HD), BF16)

    def attend(kv, chunk):
        key_parts, value_parts = [], []
        for i in range(KEY_SEGS):
            j = chunk * KEY_SEGS + i
            home = seg_ref[j]
            block = kv[(home + c) & 1, ((home >> 4) + NY - y) & 3, ((home >> 1) + NZ - z) & 7]
            seen = j < rank
            key_parts.append(twice(jnp.where(seen, block[0:BLK], stand_in)))
            value_parts.append(
                jnp.concatenate(
                    [
                        jnp.where(seen, block[BLK : 2 * BLK], nothing),
                        jnp.where(seen, ones, nothing),
                    ],
                    axis=1,
                )
            )
        key_chunk = jnp.concatenate(key_parts, axis=0)
        value_chunk = jnp.concatenate(value_parts, axis=0)
        tile = 256
        for t in range(2 * QROWS // tile):
            rows = slice(t * tile, (t + 1) * tile)
            scores = dot_t(qx[rows], key_chunk)
            old = top[rows]
            new = jnp.maximum(old, jnp.max(scores, axis=1, keepdims=True))
            top[rows] = new
            weights = jnp.exp2(scores - new).astype(BF16)
            acc[rows] = acc[rows] * jnp.exp2(old - new) + dot(weights, value_chunk)

    def attend_some(kv, low, high):
        def step(chunk, carry):
            attend(kv, chunk)
            return carry

        lax.fori_loop(low, high, step, 0)

    chunks = SEGS // KEY_SEGS
    for low in range(0, chunks, 2):
        attend_some(kv0, low, low + 2)
        run(g1, 2)
    run(g1)
    attend_some(kv1, 0, chunks)

    h0 = ring_x(me, hg0, xcp, 8)
    h1 = ring_x(me, hg1, xcp, 12)

    def finish(s):
        parts = []
        for h in range(LOCAL_HEADS):
            rows = slice(s * QROWS + h * BLK, s * QROWS + (h + 1) * BLK)
            parts.append((acc[rows, 0:HD] / acc[rows, HD : 2 * HD]).astype(BF16))
        hg[s][0] = jnp.concatenate(parts, axis=1)

    finish(0)
    run(h0, 1)
    finish(1)
    run(h1, 1)

    def project(d, begin):
        heads = jnp.concatenate([hg0[d], hg1[d]], axis=0)
        dy = (x + d + NY - y) % NY
        for j in range(NZ // 2):
            weight = jnp.concatenate(
                [
                    jnp.concatenate(
                        [wg[(k + c) % 2, dy, (2 * j + i + NZ - z) % NZ] for i in range(2)], axis=1
                    )
                    for k in range(2)
                ],
                axis=0,
            )
            lanes = slice(j * 256, (j + 1) * 256)
            term = dot(heads, weight)
            att[:, lanes] = term if begin else att[:, lanes] + term

    project(0, True)
    run(h0, 1)
    run(h1, 1)
    project(3, False)
    project(1, False)
    run(h0)
    run(h1)
    project(2, False)
    own_rows = jnp.concatenate([xg0[0], xg1[0]], axis=0)
    new_rows = own_rows.astype(F32) + gates[...] * att[...]
    out_ref[...] = jnp.where(filled == 1, new_rows, 0.0).astype(BF16)
    xcp.drain()


def on_device(tokens, norm_gain, router_weight, w_query, w_key, w_value, w_out, seg_ids, blk_ids):
    any_space = pl.BlockSpec(memory_space=pl.ANY)
    vmem = pl.BlockSpec(memory_space=pltpu.VMEM)
    smem = pl.BlockSpec(memory_space=pltpu.SMEM)
    dma = pltpu.SemaphoreType.DMA
    new_rows = pl.pallas_call(
        kernel,
        out_shape=jax.ShapeDtypeStruct((ROWS, FEATS), BF16),
        in_specs=[smem, smem, vmem, vmem, any_space, any_space, any_space, any_space, vmem],
        out_specs=vmem,
        scratch_shapes=[
            pltpu.VMEM((16, BLK, FEATS), BF16),
            pltpu.VMEM((NX, FEATS, 512), BF16),
            pltpu.VMEM((NX, FEATS, HD), BF16),
            pltpu.VMEM((NX, FEATS, HD), BF16),
            pltpu.VMEM((NX, FEATS, 2 * HD), BF16),
            pltpu.VMEM((NX, BLK, FEATS), BF16),
            pltpu.VMEM((NX, BLK, FEATS), BF16),
            pltpu.VMEM((NX, BLK, FEATS), BF16),
            pltpu.VMEM((2, 256, 128), BF16),
            pltpu.VMEM((2, 256, 128), BF16),
            pltpu.VMEM((2, NY, NZ, 256, 128), BF16),
            pltpu.VMEM((2, NY, NZ, 256, 128), BF16),
            pltpu.VMEM((2, NY, NZ, 256, 128), BF16),
            pltpu.VMEM((2 * QROWS, 2 * HD), BF16),
            pltpu.VMEM((2 * QROWS, 2 * HD), F32),
            pltpu.VMEM((2 * QROWS, 1), F32),
            pltpu.VMEM((ROWS, 1), F32),
            pltpu.VMEM((NX, BLK, 512), BF16),
            pltpu.VMEM((NX, BLK, 512), BF16),
            pltpu.VMEM((ROWS, FEATS), F32),
            dma((4,)),
            dma((2,)),
            dma((2,)),
            dma((COPIES,)),
            dma((COPIES,)),
            dma((COPIES,)),
            dma((COPIES,)),
            dma((COPIES,)),
            dma((COPIES,)),
            dma((16,)),
            dma((16,)),
        ],
        compiler_params=pltpu.CompilerParams(
            collective_id=0, has_side_effects=True, vmem_limit_bytes=56 << 20
        ),
        name="depth_layer",
    )(
        seg_ids,
        blk_ids,
        norm_gain.reshape(NX, 1, FEATS),
        router_weight.reshape(NX, 1, FEATS),
        tokens.reshape(16, BLK, FEATS),
        w_query.reshape(NX, FEATS, 512),
        w_key.reshape(NX, FEATS, HD),
        w_value.reshape(NX, FEATS, HD),
        w_out,
    )
    return new_rows.reshape(2, BLK, FEATS)


def solution(mesh):
    placed = (
        P("seq", "tp"),
        P(),
        P(),
        P(None, "tp"),
        P(None, "tp"),
        P(None, "tp"),
        P("tp", "seq"),
        P(),
        P(),
    )
    return jax.shard_map(
        on_device, mesh=mesh, in_specs=placed, out_specs=P("seq", None, "tp"), check_vma=False
    )
```

```python
import functools

import jax
import jax.numpy as jnp
from jax import lax
from jax.experimental import pallas as pl
from jax.experimental.pallas import tpu as pltpu
from jax.sharding import PartitionSpec as P

MESH = pl.DeviceIdType.MESH
F32 = jnp.float32
BF16 = jnp.bfloat16

NY, NZ, NX = 4, 8, 4
HD = 128
BLK = 128
LOCAL_HEADS = 4
ROWS = 2 * BLK
QROWS = LOCAL_HEADS * BLK
FEATS = 1024
SEGS = 32
ACC = HD + 8
KEY_SEGS = 8
Q_SCALE = 1.0 / (128.0**0.5)
MASKED = -1e30

Y_FIRST = 64
PY, PZ, RZ, RY, SIB, COPIES = 0, 4, 12, 20, 44, 56


def dot(a, b):
    return jnp.dot(a, b, preferred_element_type=F32)


def dot_t0(a, b):
    return lax.dot_general(a, b, (((0,), (0,)), ((), ())), preferred_element_type=F32)


class Place:
    def __init__(self):
        s = lax.axis_index("seq")
        self.x = lax.axis_index("tp")
        self.s = s
        self.y = s // (NZ * 2)
        self.z = (s // 2) % NZ
        self.c = s % 2

    def at(self, x=None, y=None, z=None, c=None):
        x = self.x if x is None else x
        y = self.y if y is None else y
        z = self.z if z is None else z
        c = self.c if c is None else c
        return (y * (NZ * 2) + z * 2 + c, x)


class Copies:
    def __init__(self, send_sems, recv_sems):
        self.ss, self.rs = send_sems, recv_sems
        self.made = {}

    def send(self, src, dst, k, device):
        copy = pltpu.make_async_remote_copy(
            src_ref=src,
            dst_ref=dst,
            send_sem=self.ss.at[k],
            recv_sem=self.rs.at[k],
            device_id=device,
            device_id_type=MESH,
        )
        copy.start()
        self.made[k] = copy

    def recv(self, k):
        self.made[k].wait_recv()

    def drain(self):
        for copy in self.made.values():
            copy.wait_send()
        self.made = {}


def gather_yz(me, both, cp):
    buf, other = both.at[0], both.at[1]
    up_y, down_y = me.at(y=(me.y + 1) % NY), me.at(y=(me.y + 3) % NY)
    up_z, down_z = me.at(z=(me.z + 1) % NZ), me.at(z=(me.z + 7) % NZ)
    sib = me.at(c=1 - me.c)
    half = Y_FIRST // 2
    mid = Y_FIRST + (256 - Y_FIRST) // 2

    def p(dy, lo=0, hi=Y_FIRST):
        return buf.at[dy, 0, lo:hi]

    def col(dz, lo=0, hi=Y_FIRST):
        return buf.at[:, dz, lo:hi]

    def r(dz, dy=0, lo=Y_FIRST, hi=256):
        return buf.at[dy, dz, lo:hi]

    order = (0, 7, 1, 6, 2, 5, 3, 4)

    def row_out(j):
        cp.send(r(order[j]), r(order[j], 3), RY + j, up_y)
        cp.send(r(order[j]), r(order[j], 1), RY + 8 + j, down_y)

    def row_in(j):
        cp.recv(RY + j)
        if j % 2 == 0:
            cp.send(r(order[j], 3), r(order[j], 2), RY + 16 + j, up_y)
        cp.recv(RY + 8 + j)
        if j % 2 == 1:
            cp.send(r(order[j], 1), r(order[j], 2), RY + 16 + j, down_y)

    def sib_col(j, dz):
        cp.send(col(dz), other.at[:, dz, 0:Y_FIRST], SIB + j, sib)

    def sib_row(j, dy):
        cp.send(buf.at[dy, :, Y_FIRST:256], other.at[dy, :, Y_FIRST:256], SIB + 8 + j, sib)

    cp.send(p(0), p(3), PY, up_y)
    cp.send(p(0), p(1), PY + 1, down_y)
    cp.send(r(0), r(7), RZ, up_z)
    cp.send(r(0), r(1), RZ + 1, down_z)
    row_out(0)
    yield
    cp.recv(PY)
    cp.send(p(3, 0, half), p(2, 0, half), PY + 2, up_y)
    cp.recv(PY + 1)
    cp.send(p(1, half, Y_FIRST), p(2, half, Y_FIRST), PY + 3, down_y)
    yield
    cp.recv(RZ)
    cp.send(r(7), r(6), RZ + 2, up_z)
    cp.recv(RZ + 1)
    cp.send(r(1), r(2), RZ + 3, down_z)
    row_out(1)
    row_out(2)
    yield
    cp.recv(PY + 2)
    cp.recv(PY + 3)
    cp.send(col(0), col(7), PZ, up_z)
    cp.send(col(0), col(1), PZ + 1, down_z)
    sib_col(0, 0)
    yield
    cp.recv(RZ + 2)
    cp.send(r(6), r(5), RZ + 4, up_z)
    cp.recv(RZ + 3)
    cp.send(r(2), r(3), RZ + 5, down_z)
    row_out(3)
    row_out(4)
    yield
    row_in(0)
    cp.recv(RZ + 4)
    cp.send(r(5, 0, Y_FIRST, mid), r(4, 0, Y_FIRST, mid), RZ + 6, up_z)
    cp.recv(RZ + 5)
    cp.send(r(3, 0, mid, 256), r(4, 0, mid, 256), RZ + 7, down_z)
    row_out(5)
    row_out(6)
    yield
    cp.recv(PZ)
    cp.send(col(7), col(6), PZ + 2, up_z)
    cp.recv(PZ + 1)
    cp.send(col(1), col(2), PZ + 3, down_z)
    sib_col(1, 7)
    sib_col(2, 1)
    yield
    cp.recv(RZ + 6)
    cp.recv(RZ + 7)
    row_out(7)
    sib_row(0, 0)
    row_in(1)
    row_in(2)
    yield
    cp.recv(PZ + 2)
    cp.send(col(6), col(5), PZ + 4, up_z)
    cp.recv(PZ + 3)
    cp.send(col(2), col(3), PZ + 5, down_z)
    sib_col(3, 6)
    sib_col(4, 2)
    row_in(3)
    row_in(4)
    yield
    cp.recv(PZ + 4)
    cp.send(col(5, 0, half), col(4, 0, half), PZ + 6, up_z)
    cp.recv(PZ + 5)
    cp.send(col(3, half, Y_FIRST), col(4, half, Y_FIRST), PZ + 7, down_z)
    sib_col(5, 5)
    sib_col(6, 3)
    row_in(5)
    yield
    row_in(6)
    row_in(7)
    sib_row(1, 3)
    sib_row(2, 1)
    yield
    cp.recv(PZ + 6)
    cp.recv(PZ + 7)
    sib_col(7, 4)
    for j in range(8):
        cp.recv(RY + 16 + j)
    sib_row(3, 2)
    yield
    for j in range(12):
        cp.recv(SIB + j)
    cp.drain()


def ring_x(me, buf, cp, base):
    mid = BLK // 2
    up, down = me.at(x=(me.x + 1) % NX), me.at(x=(me.x + 3) % NX)
    cp.send(buf.at[0], buf.at[3], base, up)
    cp.send(buf.at[0], buf.at[1], base + 1, down)
    yield
    cp.recv(base)
    cp.send(buf.at[3, 0:mid], buf.at[2, 0:mid], base + 2, up)
    cp.recv(base + 1)
    cp.send(buf.at[1, mid:BLK], buf.at[2, mid:BLK], base + 3, down)
    yield
    cp.recv(base + 2)
    cp.recv(base + 3)


def run(steps, count=None):
    if count is None:
        for _ in steps:
            pass
        return
    for _ in range(count):
        next(steps, None)


def kernel(
    seg_ref,
    blk_ref,
    gain_ref,
    router_ref,
    tok_ref,
    wq_hbm,
    wk_hbm,
    wv_hbm,
    wo_ref,
    out_ref,
    tok,
    wq,
    wk,
    wv,
    wkv,
    gain,
    router,
    xg0,
    xg1,
    normed0,
    normed1,
    wsend,
    wrecv,
    wg,
    kv0,
    kv1,
    qt,
    acc,
    top,
    gates,
    hg0,
    hg1,
    att,
    local_sems,
    w_ss,
    w_rs,
    gw_ss,
    gw_rs,
    g0_ss,
    g0_rs,
    g1_ss,
    g1_rs,
    x_ss,
    x_rs,
):
    me = Place()
    x, y, z, c = me.x, me.y, me.z, me.c
    xg, hg, normed = (xg0, xg1), (hg0, hg1), (normed0, normed1)
    tok_copy = pltpu.make_async_copy(tok_ref, tok, local_sems.at[0])
    wk_copy = pltpu.make_async_copy(wk_hbm, wk, local_sems.at[1])
    wv_copy = pltpu.make_async_copy(wv_hbm, wv, local_sems.at[2])
    wq_copy = pltpu.make_async_copy(wq_hbm, wq, local_sems.at[3])
    for copy in (tok_copy, wk_copy, wv_copy, wq_copy):
        copy.start()

    for small, wide in ((gain_ref, gain), (router_ref, router)):
        values = small[...].astype(F32)
        for t in range(NX):
            wide[t] = jnp.concatenate([values[t * 8 + i : t * 8 + i + 1] for i in range(8)], axis=1)

    sib = me.at(c=1 - c)
    barrier = pltpu.get_barrier_semaphore()
    neighbours = [
        me.at(x=(x + 1) % NX),
        me.at(x=(x + 3) % NX),
        me.at(y=(y + 1) % NY),
        me.at(y=(y + 3) % NY),
        me.at(z=(z + 1) % NZ),
        me.at(z=(z + 7) % NZ),
        sib,
    ]
    for device in neighbours:
        pl.semaphore_signal(barrier, 1, device_id=device, device_id_type=MESH)

    @pl.when(x != y)
    def _():
        for h in range(2):
            pl.semaphore_signal(
                barrier, 1, device_id=me.at(x=y, y=x, c=h), device_id_type=MESH
            )

    here = lax.broadcasted_iota(jnp.int32, (64, 128), 1)
    there = lax.broadcasted_iota(jnp.int32, (64, 128), 0)
    spread = jnp.where(here == there + 64 * c, 1.0, 0.0).astype(BF16)
    for h in range(2):
        wsend[h] = dot_t0(wo_ref[:, h * 256 : (h + 1) * 256], spread).astype(BF16)

    own = me.s

    def look(j, carry):
        rank, hit, first, second = carry
        seg = seg_ref[j]
        same = seg == own
        return (
            rank + jnp.where(seg < own, 1, 0),
            jnp.where(same, 1, hit),
            jnp.where(same, blk_ref[0, j], first),
            jnp.where(same, blk_ref[1, j], second),
        )

    zero = jnp.int32(0)
    rank, filled, first, second = lax.fori_loop(0, SEGS, look, (zero, zero, zero, zero))

    tok_copy.wait()
    for s, block in enumerate((first, second)):
        xg[s][0] = tok[block]

    @pl.when(x != y)
    def _():
        pl.semaphore_wait(barrier, 9)

    @pl.when(x == y)
    def _():
        pl.semaphore_wait(barrier, 7)

    xcp = Copies(x_ss, x_rs)
    x0 = ring_x(me, xg0, xcp, 0)
    x1 = ring_x(me, xg1, xcp, 4)
    run(x0, 1)
    run(x1, 1)

    def w_copy(h, slot, device):
        return pltpu.make_async_remote_copy(
            src_ref=wsend.at[h],
            dst_ref=wrecv.at[slot],
            send_sem=w_ss.at[h],
            recv_sem=w_rs.at[slot],
            device_id=device,
            device_id_type=MESH,
        )

    @pl.when(x != y)
    def _():
        for h in range(2):
            w_copy(h, c, me.at(x=y, y=x, c=h)).start()

    @pl.when(x == y)
    def _():
        w_copy(1 - c, c, sib).start()
        wrecv[c] = wsend[c]

    wk_copy.wait()
    wv_copy.wait()
    wkv[:, :, 0:HD] = wk[...]
    wkv[:, :, HD : 2 * HD] = wv[...]

    @pl.when(x != y)
    def _():
        for h in range(2):
            w_copy(h, h, me.at(x=y, y=x, c=h)).wait()

    @pl.when(x == y)
    def _():
        w_copy(1 - c, 1 - c, sib).wait()

    wg[0, 0, 0] = wrecv[0] + wrecv[1]
    gw = gather_yz(me, wg, Copies(gw_ss, gw_rs))
    run(gw, 3)

    run(x0, 1)
    run(gw, 2)
    run(x1, 1)
    run(gw, 1)

    feat = [(x + d) % NX for d in range(NX)]

    def norm(s):
        rows = slice(s * BLK, (s + 1) * BLK)
        squares = jnp.zeros((BLK, 1), F32)
        routed = jnp.zeros((BLK, 1), F32)
        for d in range(NX):
            part = xg[s][d].astype(F32)
            squares += jnp.sum(part * part, axis=1, keepdims=True)
            routed += jnp.sum(part * router[feat[d]], axis=1, keepdims=True)
        scale = lax.rsqrt(squares * (1.0 / (NX * FEATS)) + 1e-05)
        gates[rows] = jax.nn.sigmoid(routed)
        for d in range(NX):
            normed[s][d] = (xg[s][d].astype(F32) * scale * gain[feat[d]]).astype(BF16)

    def through(s, weight):
        total = dot(normed[s][0], weight[feat[0]])
        for d in range(1, NX):
            total += dot(normed[s][d], weight[feat[d]])
        return total.astype(BF16)

    def keys(s, kv):
        found = through(s, wkv)
        kv[0, 0, 0] = jnp.concatenate([found[:, 0:HD], found[:, HD : 2 * HD]], axis=0)

    def queries(s):
        found = through(s, wq).astype(F32) * Q_SCALE
        for h in range(LOCAL_HEADS):
            columns = slice(s * QROWS + h * BLK, s * QROWS + (h + 1) * BLK)
            turned = found[:, h * HD : (h + 1) * HD].T
            high = turned.astype(BF16)
            qt[0:HD, columns] = high
            qt[HD : 2 * HD, columns] = (turned - high.astype(F32)).astype(BF16)

    ones = jnp.ones((BLK, HD), BF16)

    def twice(key):
        return jnp.concatenate([key, key], axis=1)

    def weigh(scores, most, value_t):
        return dot(value_t, jnp.exp(scores - most).astype(BF16))

    def with_sum(value, mark):
        return jnp.concatenate([value.T, mark], axis=0)

    def own_blocks():
        own0, own1 = kv0[0, 0, 0], kv1[0, 0, 0]
        key0, value0 = own0[0:BLK], with_sum(own0[BLK : 2 * BLK], ones)
        key1, value1 = own1[0:BLK], with_sum(own1[BLK : 2 * BLK], ones)
        key = lax.broadcasted_iota(jnp.int32, (BLK, QROWS), 0)
        query = lax.broadcasted_iota(jnp.int32, (BLK, QROWS), 1) % BLK
        seen = key <= query
        columns = slice(0, QROWS)
        s00 = jnp.where(seen, dot(twice(key0), qt[:, columns]), MASKED)
        most = jnp.max(s00, axis=0, keepdims=True)
        top[:, columns] = most
        acc[:, columns] = weigh(s00, most, value0)[0:ACC]
        columns = slice(QROWS, 2 * QROWS)
        s10 = dot(twice(key0), qt[:, columns])
        s11 = jnp.where(seen, dot(twice(key1), qt[:, columns]), MASKED)
        most = jnp.max(jnp.maximum(s10, s11), axis=0, keepdims=True)
        top[:, columns] = most
        acc[:, columns] = (weigh(s10, most, value0) + weigh(s11, most, value1))[0:ACC]

    nothing = jnp.zeros((BLK, HD), BF16)

    def attend(kv, chunk, stand_in):
        key_parts, value_parts, marks = [], [], []
        for i in range(KEY_SEGS):
            j = chunk * KEY_SEGS + i
            home = seg_ref[j]
            block = kv[(home + c) & 1, ((home >> 4) + NY - y) & 3, ((home >> 1) + NZ - z) & 7]
            seen = j < rank
            key_parts.append(jnp.where(seen, block[0:BLK], stand_in))
            value_parts.append(jnp.where(seen, block[BLK : 2 * BLK], nothing))
            marks.append(jnp.where(seen, ones, nothing))
        key_chunk = twice(jnp.concatenate(key_parts, axis=0))
        value_t = with_sum(
            jnp.concatenate(value_parts, axis=0), jnp.concatenate(marks, axis=1)
        )
        tile = 256
        for t in range(2 * QROWS // tile):
            columns = slice(t * tile, (t + 1) * tile)
            scores = dot(key_chunk, qt[:, columns])
            old = top[:, columns]
            new = jnp.maximum(old, jnp.max(scores, axis=0, keepdims=True))
            top[:, columns] = new
            acc[:, columns] = (
                acc[:, columns] * jnp.exp(old - new) + weigh(scores, new, value_t)[0:ACC]
            )

    def attend_some(kv, low, high):
        stand_in = jnp.broadcast_to(kv0[0, 0, 0][0:1], (BLK, HD))

        def step(chunk, carry):
            attend(kv, chunk, stand_in)
            return carry

        lax.fori_loop(low, high, step, 0)

    chunks = SEGS // KEY_SEGS

    run(x0)
    norm(0)
    keys(0, kv0)
    g0 = gather_yz(me, kv0, Copies(g0_ss, g0_rs))
    run(g0, 1)
    run(gw, 2)
    run(x1)
    norm(1)
    keys(1, kv1)
    g1 = gather_yz(me, kv1, Copies(g1_ss, g1_rs))
    run(g1, 1)
    run(g0, 2)
    run(gw, 1)
    wq_copy.wait()
    queries(0)
    run(g1, 2)
    run(g0, 1)
    run(gw, 1)
    queries(1)
    run(g0, 1)
    run(g1, 1)
    run(gw, 1)
    own_blocks()
    run(g0, 1)
    run(gw, 1)
    for _ in range(4):
        run(g0, 1)
        run(g1, 1)
        run(gw, 1)
    run(g0)
    for low in range(chunks):
        attend_some(kv0, low, low + 1)
        run(g1, 2)
    run(g1)
    run(gw)
    attend_some(kv1, 0, chunks)

    h0 = ring_x(me, hg0, xcp, 8)
    h1 = ring_x(me, hg1, xcp, 12)

    def finish(s):
        parts = []
        for h in range(LOCAL_HEADS):
            columns = slice(s * QROWS + h * BLK, s * QROWS + (h + 1) * BLK)
            parts.append((acc[0:HD, columns] / acc[HD : HD + 1, columns]).T.astype(BF16))
        hg[s][0] = jnp.concatenate(parts, axis=1)

    finish(0)
    run(h0, 1)
    finish(1)
    run(h1, 1)

    def project(d, begin):
        heads = jnp.concatenate([hg0[d], hg1[d]], axis=0)
        dy = (x + d + NY - y) % NY
        for j in range(NZ // 2):
            weight = jnp.concatenate(
                [
                    jnp.concatenate(
                        [wg[(k + c) % 2, dy, (2 * j + i + NZ - z) % NZ] for i in range(2)], axis=1
                    )
                    for k in range(2)
                ],
                axis=0,
            )
            lanes = slice(j * 256, (j + 1) * 256)
            term = dot(heads, weight)
            att[:, lanes] = term if begin else att[:, lanes] + term

    project(0, True)
    run(h0, 1)
    run(h1, 1)
    project(3, False)
    project(1, False)
    run(h0)
    run(h1)
    project(2, False)
    own_rows = jnp.concatenate([xg0[0], xg1[0]], axis=0)
    new_rows = own_rows.astype(F32) + gates[...] * att[...]
    out_ref[...] = jnp.where(filled == 1, new_rows, 0.0).astype(BF16)
    xcp.drain()


def on_device(tokens, norm_gain, router_weight, w_query, w_key, w_value, w_out, seg_ids, blk_ids):
    any_space = pl.BlockSpec(memory_space=pl.ANY)
    vmem = pl.BlockSpec(memory_space=pltpu.VMEM)
    smem = pl.BlockSpec(memory_space=pltpu.SMEM)
    dma = pltpu.SemaphoreType.DMA
    new_rows = pl.pallas_call(
        kernel,
        out_shape=jax.ShapeDtypeStruct((ROWS, FEATS), BF16),
        in_specs=[smem, smem, vmem, vmem, any_space, any_space, any_space, any_space, vmem],
        out_specs=vmem,
        scratch_shapes=[
            pltpu.VMEM((16, BLK, FEATS), BF16),
            pltpu.VMEM((NX, FEATS, 512), BF16),
            pltpu.VMEM((NX, FEATS, HD), BF16),
            pltpu.VMEM((NX, FEATS, HD), BF16),
            pltpu.VMEM((NX, FEATS, 2 * HD), BF16),
            pltpu.VMEM((NX, 1, FEATS), F32),
            pltpu.VMEM((NX, 1, FEATS), F32),
            pltpu.VMEM((NX, BLK, FEATS), BF16),
            pltpu.VMEM((NX, BLK, FEATS), BF16),
            pltpu.VMEM((NX, BLK, FEATS), BF16),
            pltpu.VMEM((NX, BLK, FEATS), BF16),
            pltpu.VMEM((2, 256, 128), BF16),
            pltpu.VMEM((2, 256, 128), BF16),
            pltpu.VMEM((2, NY, NZ, 256, 128), BF16),
            pltpu.VMEM((2, NY, NZ, 256, 128), BF16),
            pltpu.VMEM((2, NY, NZ, 256, 128), BF16),
            pltpu.VMEM((2 * HD, 2 * QROWS), BF16),
            pltpu.VMEM((ACC, 2 * QROWS), F32),
            pltpu.VMEM((1, 2 * QROWS), F32),
            pltpu.VMEM((ROWS, 1), F32),
            pltpu.VMEM((NX, BLK, 512), BF16),
            pltpu.VMEM((NX, BLK, 512), BF16),
            pltpu.VMEM((ROWS, FEATS), F32),
            dma((4,)),
            dma((2,)),
            dma((2,)),
            dma((COPIES,)),
            dma((COPIES,)),
            dma((COPIES,)),
            dma((COPIES,)),
            dma((COPIES,)),
            dma((COPIES,)),
            dma((16,)),
            dma((16,)),
        ],
        compiler_params=pltpu.CompilerParams(
            collective_id=0, has_side_effects=True, vmem_limit_bytes=56 << 20
        ),
        name="depth_layer",
    )(
        seg_ids,
        blk_ids.T,
        norm_gain.reshape(NX * 8, HD),
        router_weight.reshape(NX * 8, HD),
        tokens.reshape(16, BLK, FEATS),
        w_query.reshape(NX, FEATS, 512),
        w_key.reshape(NX, FEATS, HD),
        w_value.reshape(NX, FEATS, HD),
        w_out.T,
    )
    return new_rows.reshape(2, BLK, FEATS)


def solution(mesh):
    placed = (
        P("seq", "tp"),
        P(),
        P(),
        P(None, "tp"),
        P(None, "tp"),
        P(None, "tp"),
        P("tp", "seq"),
        P(),
        P(),
    )
    return jax.shard_map(
        on_device, mesh=mesh, in_specs=placed, out_specs=P("seq", None, "tp"), check_vma=False
    )
```

```python
import functools

import jax
import jax.numpy as jnp
from jax import lax
from jax.experimental import pallas as pl
from jax.experimental.pallas import tpu as pltpu
from jax.sharding import PartitionSpec as P

MESH = pl.DeviceIdType.MESH
F32 = jnp.float32
BF16 = jnp.bfloat16

NY, NZ, NX = 4, 8, 4
HD = 128
BLK = 128
LOCAL_HEADS = 4
ROWS = 2 * BLK
QROWS = LOCAL_HEADS * BLK
FEATS = 1024
SEGS = 32
ACC = HD + 8
KEY_SEGS = 8
Q_SCALE = 1.0 / (128.0**0.5)
MASKED = -1e30

Y_FIRST = 64
PY, PZ, RZ, RY, SIB, COPIES = 0, 4, 12, 20, 44, 56


def dot(a, b):
    return jnp.dot(a, b, preferred_element_type=F32)


def dot_t0(a, b):
    return lax.dot_general(a, b, (((0,), (0,)), ((), ())), preferred_element_type=F32)


class Place:
    def __init__(self):
        s = lax.axis_index("seq")
        self.x = lax.axis_index("tp")
        self.s = s
        self.y = s // (NZ * 2)
        self.z = (s // 2) % NZ
        self.c = s % 2

    def at(self, x=None, y=None, z=None, c=None):
        x = self.x if x is None else x
        y = self.y if y is None else y
        z = self.z if z is None else z
        c = self.c if c is None else c
        return (y * (NZ * 2) + z * 2 + c, x)


class Copies:
    def __init__(self, send_sems, recv_sems):
        self.ss, self.rs = send_sems, recv_sems
        self.made = {}

    def send(self, src, dst, k, device):
        copy = pltpu.make_async_remote_copy(
            src_ref=src,
            dst_ref=dst,
            send_sem=self.ss.at[k],
            recv_sem=self.rs.at[k],
            device_id=device,
            device_id_type=MESH,
        )
        copy.start()
        self.made[k] = copy

    def recv(self, k):
        self.made[k].wait_recv()

    def drain(self):
        for copy in self.made.values():
            copy.wait_send()
        self.made = {}


def gather_yz(me, both, cp):
    buf, other = both.at[0], both.at[1]
    up_y, down_y = me.at(y=(me.y + 1) % NY), me.at(y=(me.y + 3) % NY)
    up_z, down_z = me.at(z=(me.z + 1) % NZ), me.at(z=(me.z + 7) % NZ)
    sib = me.at(c=1 - me.c)
    half = Y_FIRST // 2
    mid = Y_FIRST + (256 - Y_FIRST) // 2

    def p(dy, lo=0, hi=Y_FIRST):
        return buf.at[dy, 0, lo:hi]

    def col(dz, lo=0, hi=Y_FIRST):
        return buf.at[:, dz, lo:hi]

    def r(dz, dy=0, lo=Y_FIRST, hi=256):
        return buf.at[dy, dz, lo:hi]

    order = (0, 7, 1, 6, 2, 5, 3, 4)

    def row_out(j):
        cp.send(r(order[j]), r(order[j], 3), RY + j, up_y)
        cp.send(r(order[j]), r(order[j], 1), RY + 8 + j, down_y)

    def row_in(j):
        cp.recv(RY + j)
        if j % 2 == 0:
            cp.send(r(order[j], 3), r(order[j], 2), RY + 16 + j, up_y)
        cp.recv(RY + 8 + j)
        if j % 2 == 1:
            cp.send(r(order[j], 1), r(order[j], 2), RY + 16 + j, down_y)

    def sib_col(j, dz):
        cp.send(col(dz), other.at[:, dz, 0:Y_FIRST], SIB + j, sib)

    def sib_row(j, dy):
        cp.send(buf.at[dy, :, Y_FIRST:256], other.at[dy, :, Y_FIRST:256], SIB + 8 + j, sib)

    cp.send(p(0), p(3), PY, up_y)
    cp.send(p(0), p(1), PY + 1, down_y)
    cp.send(r(0), r(7), RZ, up_z)
    cp.send(r(0), r(1), RZ + 1, down_z)
    row_out(0)
    yield
    cp.recv(PY)
    cp.send(p(3, 0, half), p(2, 0, half), PY + 2, up_y)
    cp.recv(PY + 1)
    cp.send(p(1, half, Y_FIRST), p(2, half, Y_FIRST), PY + 3, down_y)
    yield
    cp.recv(RZ)
    cp.send(r(7), r(6), RZ + 2, up_z)
    cp.recv(RZ + 1)
    cp.send(r(1), r(2), RZ + 3, down_z)
    row_out(1)
    row_out(2)
    yield
    cp.recv(PY + 2)
    cp.recv(PY + 3)
    cp.send(col(0), col(7), PZ, up_z)
    cp.send(col(0), col(1), PZ + 1, down_z)
    sib_col(0, 0)
    yield
    cp.recv(RZ + 2)
    cp.send(r(6), r(5), RZ + 4, up_z)
    cp.recv(RZ + 3)
    cp.send(r(2), r(3), RZ + 5, down_z)
    row_out(3)
    row_out(4)
    yield
    row_in(0)
    cp.recv(RZ + 4)
    cp.send(r(5, 0, Y_FIRST, mid), r(4, 0, Y_FIRST, mid), RZ + 6, up_z)
    cp.recv(RZ + 5)
    cp.send(r(3, 0, mid, 256), r(4, 0, mid, 256), RZ + 7, down_z)
    row_out(5)
    row_out(6)
    yield
    cp.recv(PZ)
    cp.send(col(7), col(6), PZ + 2, up_z)
    cp.recv(PZ + 1)
    cp.send(col(1), col(2), PZ + 3, down_z)
    sib_col(1, 7)
    sib_col(2, 1)
    yield
    cp.recv(RZ + 6)
    cp.recv(RZ + 7)
    row_out(7)
    sib_row(0, 0)
    row_in(1)
    row_in(2)
    yield
    cp.recv(PZ + 2)
    cp.send(col(6), col(5), PZ + 4, up_z)
    cp.recv(PZ + 3)
    cp.send(col(2), col(3), PZ + 5, down_z)
    sib_col(3, 6)
    sib_col(4, 2)
    row_in(3)
    row_in(4)
    yield
    cp.recv(PZ + 4)
    cp.send(col(5, 0, half), col(4, 0, half), PZ + 6, up_z)
    cp.recv(PZ + 5)
    cp.send(col(3, half, Y_FIRST), col(4, half, Y_FIRST), PZ + 7, down_z)
    sib_col(5, 5)
    sib_col(6, 3)
    row_in(5)
    yield
    row_in(6)
    row_in(7)
    sib_row(1, 3)
    sib_row(2, 1)
    yield
    cp.recv(PZ + 6)
    cp.recv(PZ + 7)
    sib_col(7, 4)
    for j in range(8):
        cp.recv(RY + 16 + j)
    sib_row(3, 2)
    yield
    for j in range(12):
        cp.recv(SIB + j)
    cp.drain()


def ring_x(me, buf, cp, base):
    mid = BLK // 2
    up, down = me.at(x=(me.x + 1) % NX), me.at(x=(me.x + 3) % NX)
    cp.send(buf.at[0], buf.at[3], base, up)
    cp.send(buf.at[0], buf.at[1], base + 1, down)
    yield
    cp.recv(base)
    cp.send(buf.at[3, 0:mid], buf.at[2, 0:mid], base + 2, up)
    cp.recv(base + 1)
    cp.send(buf.at[1, mid:BLK], buf.at[2, mid:BLK], base + 3, down)
    yield
    cp.recv(base + 2)
    cp.recv(base + 3)


def run(steps, count=None):
    if count is None:
        for _ in steps:
            pass
        return
    for _ in range(count):
        next(steps, None)


def kernel(
    seg_ref,
    blk_ref,
    gain_ref,
    router_ref,
    tok_ref,
    wq_hbm,
    wk_hbm,
    wv_hbm,
    wo_ref,
    out_ref,
    tok,
    wq,
    wk,
    wv,
    wkv,
    gain,
    router,
    xg0,
    xg1,
    normed0,
    normed1,
    wsend,
    wrecv,
    wg,
    kv0,
    kv1,
    qt,
    acc,
    top,
    gates,
    hg0,
    hg1,
    att,
    local_sems,
    w_ss,
    w_rs,
    gw_ss,
    gw_rs,
    g0_ss,
    g0_rs,
    g1_ss,
    g1_rs,
    x_ss,
    x_rs,
):
    me = Place()
    x, y, z, c = me.x, me.y, me.z, me.c
    xg, hg, normed = (xg0, xg1), (hg0, hg1), (normed0, normed1)
    tok_copy = pltpu.make_async_copy(tok_ref, tok, local_sems.at[0])
    wk_copy = pltpu.make_async_copy(wk_hbm, wk, local_sems.at[1])
    wv_copy = pltpu.make_async_copy(wv_hbm, wv, local_sems.at[2])
    wq_copy = pltpu.make_async_copy(wq_hbm, wq, local_sems.at[3])
    for copy in (tok_copy, wk_copy, wv_copy, wq_copy):
        copy.start()

    for small, wide in ((gain_ref, gain), (router_ref, router)):
        values = small[...].astype(F32)
        for t in range(NX):
            wide[t] = jnp.concatenate([values[t * 8 + i : t * 8 + i + 1] for i in range(8)], axis=1)

    sib = me.at(c=1 - c)
    barrier = pltpu.get_barrier_semaphore()
    neighbours = [
        me.at(x=(x + 1) % NX),
        me.at(x=(x + 3) % NX),
        me.at(y=(y + 1) % NY),
        me.at(y=(y + 3) % NY),
        me.at(z=(z + 1) % NZ),
        me.at(z=(z + 7) % NZ),
        sib,
    ]
    for device in neighbours:
        pl.semaphore_signal(barrier, 1, device_id=device, device_id_type=MESH)

    @pl.when(x != y)
    def _():
        for h in range(2):
            pl.semaphore_signal(
                barrier, 1, device_id=me.at(x=y, y=x, c=h), device_id_type=MESH
            )

    here = lax.broadcasted_iota(jnp.int32, (64, 128), 1)
    there = lax.broadcasted_iota(jnp.int32, (64, 128), 0)
    spread = jnp.where(here == there + 64 * c, 1.0, 0.0).astype(BF16)
    for h in range(2):
        wsend[h] = dot_t0(wo_ref[:, h * 256 : (h + 1) * 256], spread).astype(BF16)

    own = me.s

    def look(j, carry):
        rank, hit, first, second = carry
        seg = seg_ref[j]
        same = seg == own
        return (
            rank + jnp.where(seg < own, 1, 0),
            jnp.where(same, 1, hit),
            jnp.where(same, blk_ref[0, j], first),
            jnp.where(same, blk_ref[1, j], second),
        )

    zero = jnp.int32(0)
    rank, filled, first, second = lax.fori_loop(0, SEGS, look, (zero, zero, zero, zero))

    tok_copy.wait()
    for s, block in enumerate((first, second)):
        xg[s][0] = tok[block]

    @pl.when(x != y)
    def _():
        pl.semaphore_wait(barrier, 9)

    @pl.when(x == y)
    def _():
        pl.semaphore_wait(barrier, 7)

    xcp = Copies(x_ss, x_rs)
    x0 = ring_x(me, xg0, xcp, 0)
    x1 = ring_x(me, xg1, xcp, 4)
    run(x0, 1)
    run(x1, 1)

    def w_copy(h, slot, device):
        return pltpu.make_async_remote_copy(
            src_ref=wsend.at[h],
            dst_ref=wrecv.at[slot],
            send_sem=w_ss.at[h],
            recv_sem=w_rs.at[slot],
            device_id=device,
            device_id_type=MESH,
        )

    @pl.when(x != y)
    def _():
        for h in range(2):
            w_copy(h, c, me.at(x=y, y=x, c=h)).start()

    @pl.when(x == y)
    def _():
        w_copy(1 - c, c, sib).start()
        wrecv[c] = wsend[c]

    wk_copy.wait()
    wv_copy.wait()
    wkv[:, :, 0:HD] = wk[...]
    wkv[:, :, HD : 2 * HD] = wv[...]

    @pl.when(x != y)
    def _():
        for h in range(2):
            w_copy(h, h, me.at(x=y, y=x, c=h)).wait()

    @pl.when(x == y)
    def _():
        w_copy(1 - c, 1 - c, sib).wait()

    wg[0, 0, 0] = wrecv[0] + wrecv[1]
    gw = gather_yz(me, wg, Copies(gw_ss, gw_rs))
    run(gw, 3)

    run(x0, 1)
    run(gw, 2)
    run(x1, 1)
    run(gw, 1)

    feat = [(x + d) % NX for d in range(NX)]

    def norm(s):
        rows = slice(s * BLK, (s + 1) * BLK)
        squares = jnp.zeros((BLK, 1), F32)
        routed = jnp.zeros((BLK, 1), F32)
        for d in range(NX):
            part = xg[s][d].astype(F32)
            squares += jnp.sum(part * part, axis=1, keepdims=True)
            routed += jnp.sum(part * router[feat[d]], axis=1, keepdims=True)
        scale = lax.rsqrt(squares * (1.0 / (NX * FEATS)) + 1e-05)
        gates[rows] = jax.nn.sigmoid(routed)
        for d in range(NX):
            normed[s][d] = (xg[s][d].astype(F32) * scale * gain[feat[d]]).astype(BF16)

    def through(s, weight):
        total = dot(normed[s][0], weight[feat[0]])
        for d in range(1, NX):
            total += dot(normed[s][d], weight[feat[d]])
        return total.astype(BF16)

    def keys(s, kv):
        found = through(s, wkv)
        kv[0, 0, 0] = jnp.concatenate(
            [found[:, 0:HD], found[:, HD : 2 * HD].astype(F32).T.astype(BF16)], axis=0
        )

    def queries(s):
        found = through(s, wq).astype(F32) * Q_SCALE
        for h in range(LOCAL_HEADS):
            columns = slice(s * QROWS + h * BLK, s * QROWS + (h + 1) * BLK)
            turned = found[:, h * HD : (h + 1) * HD].T
            high = turned.astype(BF16)
            qt[0:HD, columns] = high
            qt[HD : 2 * HD, columns] = (turned - high.astype(F32)).astype(BF16)

    ones = jnp.ones((BLK, HD), BF16)

    def twice(key):
        return jnp.concatenate([key, key], axis=1)

    def weigh(scores, most, value_t):
        return dot(value_t, jnp.exp(scores - most).astype(BF16))

    def with_sum(value, mark):
        return jnp.concatenate([value, mark], axis=0)

    def own_blocks():
        own0, own1 = kv0[0, 0, 0], kv1[0, 0, 0]
        key0, value0 = own0[0:BLK], with_sum(own0[BLK : 2 * BLK], ones)
        key1, value1 = own1[0:BLK], with_sum(own1[BLK : 2 * BLK], ones)
        key = lax.broadcasted_iota(jnp.int32, (BLK, QROWS), 0)
        query = lax.broadcasted_iota(jnp.int32, (BLK, QROWS), 1) % BLK
        seen = key <= query
        columns = slice(0, QROWS)
        s00 = jnp.where(seen, dot(twice(key0), qt[:, columns]), MASKED)
        most = jnp.max(s00, axis=0, keepdims=True)
        top[:, columns] = most
        acc[:, columns] = weigh(s00, most, value0)[0:ACC]
        columns = slice(QROWS, 2 * QROWS)
        s10 = dot(twice(key0), qt[:, columns])
        s11 = jnp.where(seen, dot(twice(key1), qt[:, columns]), MASKED)
        most = jnp.max(jnp.maximum(s10, s11), axis=0, keepdims=True)
        top[:, columns] = most
        acc[:, columns] = (weigh(s10, most, value0) + weigh(s11, most, value1))[0:ACC]

    nothing = jnp.zeros((BLK, HD), BF16)

    def attend(kv, chunk, stand_in):
        key_parts, value_parts, marks = [], [], []
        for i in range(KEY_SEGS):
            j = chunk * KEY_SEGS + i
            home = seg_ref[j]
            block = kv[(home + c) & 1, ((home >> 4) + NY - y) & 3, ((home >> 1) + NZ - z) & 7]
            seen = j < rank
            key_parts.append(jnp.where(seen, block[0:BLK], stand_in))
            value_parts.append(jnp.where(seen, block[BLK : 2 * BLK], nothing))
            marks.append(jnp.where(seen, ones, nothing))
        key_chunk = twice(jnp.concatenate(key_parts, axis=0))
        value_t = with_sum(
            jnp.concatenate(value_parts, axis=1), jnp.concatenate(marks, axis=1)
        )
        tile = 256
        for t in range(2 * QROWS // tile):
            columns = slice(t * tile, (t + 1) * tile)
            scores = dot(key_chunk, qt[:, columns])
            old = top[:, columns]
            new = jnp.maximum(old, jnp.max(scores, axis=0, keepdims=True))
            top[:, columns] = new
            acc[:, columns] = (
                acc[:, columns] * jnp.exp(old - new) + weigh(scores, new, value_t)[0:ACC]
            )

    def attend_some(kv, low, high):
        stand_in = jnp.broadcast_to(kv0[0, 0, 0][0:1], (BLK, HD))

        def step(chunk, carry):
            attend(kv, chunk, stand_in)
            return carry

        lax.fori_loop(low, high, step, 0)

    chunks = SEGS // KEY_SEGS

    run(x0)
    norm(0)
    keys(0, kv0)
    g0 = gather_yz(me, kv0, Copies(g0_ss, g0_rs))
    run(g0, 1)
    wq_copy.wait()
    queries(0)
    run(gw, 2)
    run(x1)
    norm(1)
    keys(1, kv1)
    g1 = gather_yz(me, kv1, Copies(g1_ss, g1_rs))
    run(g1, 1)
    run(g0, 2)
    run(gw, 1)
    run(g1, 2)
    run(g0, 1)
    run(gw, 1)
    queries(1)
    run(g0, 1)
    run(g1, 1)
    run(gw, 1)
    run(g0, 1)
    run(gw, 1)
    for _ in range(4):
        run(g0, 1)
        run(g1, 1)
        run(gw, 1)
    own_blocks()
    run(g0)
    for low in range(chunks):
        attend_some(kv0, low, low + 1)
        run(g1, 2)
    run(g1)
    run(gw)
    attend_some(kv1, 0, chunks)

    h0 = ring_x(me, hg0, xcp, 8)
    h1 = ring_x(me, hg1, xcp, 12)

    def finish(s):
        parts = []
        for h in range(LOCAL_HEADS):
            columns = slice(s * QROWS + h * BLK, s * QROWS + (h + 1) * BLK)
            parts.append((acc[0:HD, columns] / acc[HD : HD + 1, columns]).T.astype(BF16))
        hg[s][0] = jnp.concatenate(parts, axis=1)

    finish(0)
    run(h0, 1)
    finish(1)
    run(h1, 1)

    def project(d, begin):
        heads = jnp.concatenate([hg0[d], hg1[d]], axis=0)
        dy = (x + d + NY - y) % NY
        for j in range(NZ // 2):
            weight = jnp.concatenate(
                [
                    jnp.concatenate(
                        [wg[(k + c) % 2, dy, (2 * j + i + NZ - z) % NZ] for i in range(2)], axis=1
                    )
                    for k in range(2)
                ],
                axis=0,
            )
            lanes = slice(j * 256, (j + 1) * 256)
            term = dot(heads, weight)
            att[:, lanes] = term if begin else att[:, lanes] + term

    project(0, True)
    run(h0, 1)
    run(h1, 1)
    project(3, False)
    project(1, False)
    run(h0)
    run(h1)
    project(2, False)
    own_rows = jnp.concatenate([xg0[0], xg1[0]], axis=0)
    new_rows = own_rows.astype(F32) + gates[...] * att[...]
    out_ref[...] = jnp.where(filled == 1, new_rows, 0.0).astype(BF16)
    xcp.drain()


def on_device(tokens, norm_gain, router_weight, w_query, w_key, w_value, w_out, seg_ids, blk_ids):
    any_space = pl.BlockSpec(memory_space=pl.ANY)
    vmem = pl.BlockSpec(memory_space=pltpu.VMEM)
    smem = pl.BlockSpec(memory_space=pltpu.SMEM)
    dma = pltpu.SemaphoreType.DMA
    new_rows = pl.pallas_call(
        kernel,
        out_shape=jax.ShapeDtypeStruct((ROWS, FEATS), BF16),
        in_specs=[smem, smem, vmem, vmem, any_space, any_space, any_space, any_space, vmem],
        out_specs=vmem,
        scratch_shapes=[
            pltpu.VMEM((16, BLK, FEATS), BF16),
            pltpu.VMEM((NX, FEATS, 512), BF16),
            pltpu.VMEM((NX, FEATS, HD), BF16),
            pltpu.VMEM((NX, FEATS, HD), BF16),
            pltpu.VMEM((NX, FEATS, 2 * HD), BF16),
            pltpu.VMEM((NX, 1, FEATS), F32),
            pltpu.VMEM((NX, 1, FEATS), F32),
            pltpu.VMEM((NX, BLK, FEATS), BF16),
            pltpu.VMEM((NX, BLK, FEATS), BF16),
            pltpu.VMEM((NX, BLK, FEATS), BF16),
            pltpu.VMEM((NX, BLK, FEATS), BF16),
            pltpu.VMEM((2, 256, 128), BF16),
            pltpu.VMEM((2, 256, 128), BF16),
            pltpu.VMEM((2, NY, NZ, 256, 128), BF16),
            pltpu.VMEM((2, NY, NZ, 256, 128), BF16),
            pltpu.VMEM((2, NY, NZ, 256, 128), BF16),
            pltpu.VMEM((2 * HD, 2 * QROWS), BF16),
            pltpu.VMEM((ACC, 2 * QROWS), F32),
            pltpu.VMEM((1, 2 * QROWS), F32),
            pltpu.VMEM((ROWS, 1), F32),
            pltpu.VMEM((NX, BLK, 512), BF16),
            pltpu.VMEM((NX, BLK, 512), BF16),
            pltpu.VMEM((ROWS, FEATS), F32),
            dma((4,)),
            dma((2,)),
            dma((2,)),
            dma((COPIES,)),
            dma((COPIES,)),
            dma((COPIES,)),
            dma((COPIES,)),
            dma((COPIES,)),
            dma((COPIES,)),
            dma((16,)),
            dma((16,)),
        ],
        compiler_params=pltpu.CompilerParams(
            collective_id=0, has_side_effects=True, vmem_limit_bytes=56 << 20
        ),
        name="depth_layer",
    )(
        seg_ids,
        blk_ids.T,
        norm_gain.reshape(NX * 8, HD),
        router_weight.reshape(NX * 8, HD),
        tokens.reshape(16, BLK, FEATS),
        w_query.reshape(NX, FEATS, 512),
        w_key.reshape(NX, FEATS, HD),
        w_value.reshape(NX, FEATS, HD),
        w_out.T,
    )
    return new_rows.reshape(2, BLK, FEATS)


def solution(mesh):
    placed = (
        P("seq", "tp"),
        P(),
        P(),
        P(None, "tp"),
        P(None, "tp"),
        P(None, "tp"),
        P("tp", "seq"),
        P(),
        P(),
    )
    return jax.shard_map(
        on_device, mesh=mesh, in_specs=placed, out_specs=P("seq", None, "tp"), check_vma=False
    )
```

```python
import functools

import jax
import jax.numpy as jnp
from jax import lax
from jax.experimental import pallas as pl
from jax.experimental.pallas import tpu as pltpu
from jax.sharding import PartitionSpec as P

MESH = pl.DeviceIdType.MESH
F32 = jnp.float32
BF16 = jnp.bfloat16

NY, NZ, NX = 4, 8, 4
HD = 128
BLK = 128
LOCAL_HEADS = 4
ROWS = 2 * BLK
QROWS = LOCAL_HEADS * BLK
FEATS = 1024
SEGS = 32
ACC = HD + 8
KEY_SEGS = 8
Q_SCALE = 1.0 / (128.0**0.5)
MASKED = -1e30

Y_FIRST = 64
PY, PZ, RZ, RY, SIB, COPIES = 0, 4, 12, 20, 44, 63


def dot(a, b):
    return jnp.dot(a, b, preferred_element_type=F32)


def dot_t0(a, b):
    return lax.dot_general(a, b, (((0,), (0,)), ((), ())), preferred_element_type=F32)


class Place:
    def __init__(self):
        s = lax.axis_index("seq")
        self.x = lax.axis_index("tp")
        self.s = s
        self.y = s // (NZ * 2)
        self.z = (s // 2) % NZ
        self.c = s % 2

    def at(self, x=None, y=None, z=None, c=None):
        x = self.x if x is None else x
        y = self.y if y is None else y
        z = self.z if z is None else z
        c = self.c if c is None else c
        return (y * (NZ * 2) + z * 2 + c, x)


class Copies:
    def __init__(self, send_sems, recv_sems):
        self.ss, self.rs = send_sems, recv_sems
        self.made = {}

    def send(self, src, dst, k, device):
        copy = pltpu.make_async_remote_copy(
            src_ref=src,
            dst_ref=dst,
            send_sem=self.ss.at[k],
            recv_sem=self.rs.at[k],
            device_id=device,
            device_id_type=MESH,
        )
        copy.start()
        self.made[k] = copy

    def recv(self, k):
        self.made[k].wait_recv()

    def drain(self):
        for copy in self.made.values():
            copy.wait_send()
        self.made = {}


def gather_yz(me, both, cp):
    buf, other = both.at[0], both.at[1]
    up_y, down_y = me.at(y=(me.y + 1) % NY), me.at(y=(me.y + 3) % NY)
    up_z, down_z = me.at(z=(me.z + 1) % NZ), me.at(z=(me.z + 7) % NZ)
    sib = me.at(c=1 - me.c)
    half = Y_FIRST // 2
    mid = Y_FIRST + (256 - Y_FIRST) // 2

    def p(dy, lo=0, hi=Y_FIRST):
        return buf.at[dy, 0, lo:hi]

    def col(dz, lo=0, hi=Y_FIRST):
        return buf.at[:, dz, lo:hi]

    def r(dz, dy=0, lo=Y_FIRST, hi=256):
        return buf.at[dy, dz, lo:hi]

    order = (0, 7, 1, 6, 2, 5, 3, 4)

    def row_out(j):
        cp.send(r(order[j]), r(order[j], 3), RY + j, up_y)
        cp.send(r(order[j]), r(order[j], 1), RY + 8 + j, down_y)

    def row_in(j):
        cp.recv(RY + j)
        if j % 2 == 0:
            cp.send(r(order[j], 3), r(order[j], 2), RY + 16 + j, up_y)
        cp.recv(RY + 8 + j)
        if j % 2 == 1:
            cp.send(r(order[j], 1), r(order[j], 2), RY + 16 + j, down_y)

    def sib_col(j, dz):
        cp.send(col(dz), other.at[:, dz, 0:Y_FIRST], SIB + j, sib)

    def sib_row(j, dy):
        cp.send(buf.at[dy, :, Y_FIRST:256], other.at[dy, :, Y_FIRST:256], SIB + 8 + j, sib)

    cp.send(p(0), p(3), PY, up_y)
    cp.send(p(0), p(1), PY + 1, down_y)
    cp.send(r(0), r(7), RZ, up_z)
    cp.send(r(0), r(1), RZ + 1, down_z)
    row_out(0)
    yield
    cp.recv(PY)
    cp.send(p(3, 0, half), p(2, 0, half), PY + 2, up_y)
    cp.recv(PY + 1)
    cp.send(p(1, half, Y_FIRST), p(2, half, Y_FIRST), PY + 3, down_y)
    yield
    cp.recv(RZ)
    cp.send(r(7), r(6), RZ + 2, up_z)
    cp.recv(RZ + 1)
    cp.send(r(1), r(2), RZ + 3, down_z)
    row_out(1)
    row_out(2)
    yield
    cp.recv(PY + 2)
    cp.recv(PY + 3)
    cp.send(col(0), col(7), PZ, up_z)
    cp.send(col(0), col(1), PZ + 1, down_z)
    sib_col(0, 0)
    yield
    cp.recv(RZ + 2)
    cp.send(r(6), r(5), RZ + 4, up_z)
    cp.recv(RZ + 3)
    cp.send(r(2), r(3), RZ + 5, down_z)
    row_out(3)
    row_out(4)
    yield
    row_in(0)
    cp.recv(RZ + 4)
    cp.send(r(5, 0, Y_FIRST, mid), r(4, 0, Y_FIRST, mid), RZ + 6, up_z)
    cp.recv(RZ + 5)
    cp.send(r(3, 0, mid, 256), r(4, 0, mid, 256), RZ + 7, down_z)
    row_out(5)
    row_out(6)
    yield
    cp.recv(PZ)
    cp.send(col(7), col(6), PZ + 2, up_z)
    cp.recv(PZ + 1)
    cp.send(col(1), col(2), PZ + 3, down_z)
    sib_col(1, 7)
    sib_col(2, 1)
    yield
    cp.recv(RZ + 6)
    cp.recv(RZ + 7)
    row_out(7)
    sib_row(0, 0)
    row_in(1)
    row_in(2)
    yield
    cp.recv(PZ + 2)
    cp.send(col(6), col(5), PZ + 4, up_z)
    cp.recv(PZ + 3)
    cp.send(col(2), col(3), PZ + 5, down_z)
    sib_col(3, 6)
    sib_col(4, 2)
    row_in(3)
    row_in(4)
    yield
    cp.recv(PZ + 4)
    cp.send(col(5, 0, half), col(4, 0, half), PZ + 6, up_z)
    cp.recv(PZ + 5)
    cp.send(col(3, half, Y_FIRST), col(4, half, Y_FIRST), PZ + 7, down_z)
    sib_col(5, 5)
    sib_col(6, 3)
    row_in(5)
    yield
    row_in(6)
    row_in(7)
    sib_row(1, 3)
    sib_row(2, 1)
    yield
    cp.recv(PZ + 6)
    cp.recv(PZ + 7)
    sib_col(7, 4)
    for j in range(8):
        cp.recv(RY + 16 + j)
        far = r(order[j], 2)
        cp.send(far, other.at[2, order[j], Y_FIRST:256], SIB + 11 + j, sib)
    yield
    for j in range(19):
        cp.recv(SIB + j)
    cp.drain()


def ring_x(me, buf, cp, base):
    mid = BLK // 2
    up, down = me.at(x=(me.x + 1) % NX), me.at(x=(me.x + 3) % NX)
    cp.send(buf.at[0], buf.at[3], base, up)
    cp.send(buf.at[0], buf.at[1], base + 1, down)
    yield
    cp.recv(base)
    cp.send(buf.at[3, 0:mid], buf.at[2, 0:mid], base + 2, up)
    cp.recv(base + 1)
    cp.send(buf.at[1, mid:BLK], buf.at[2, mid:BLK], base + 3, down)
    yield
    cp.recv(base + 2)
    cp.recv(base + 3)


def run(steps, count=None):
    if count is None:
        for _ in steps:
            pass
        return
    for _ in range(count):
        next(steps, None)


def kernel(
    seg_ref,
    blk_ref,
    gain_ref,
    router_ref,
    tok_ref,
    wq_hbm,
    wk_hbm,
    wv_hbm,
    wo_ref,
    out_ref,
    tok,
    wq,
    wk,
    wv,
    wkv,
    gain,
    router,
    xg0,
    xg1,
    normed0,
    normed1,
    wsend,
    wrecv,
    wg,
    kv0,
    kv1,
    qt,
    acc,
    top,
    gates,
    hg0,
    hg1,
    att,
    local_sems,
    w_ss,
    w_rs,
    gw_ss,
    gw_rs,
    g0_ss,
    g0_rs,
    g1_ss,
    g1_rs,
    x_ss,
    x_rs,
):
    me = Place()
    x, y, z, c = me.x, me.y, me.z, me.c
    xg, hg, normed = (xg0, xg1), (hg0, hg1), (normed0, normed1)
    tok_copy = pltpu.make_async_copy(tok_ref, tok, local_sems.at[0])
    wk_copy = pltpu.make_async_copy(wk_hbm, wk, local_sems.at[1])
    wv_copy = pltpu.make_async_copy(wv_hbm, wv, local_sems.at[2])
    wq_copy = pltpu.make_async_copy(wq_hbm, wq, local_sems.at[3])
    for copy in (tok_copy, wk_copy, wv_copy, wq_copy):
        copy.start()

    for small, wide in ((gain_ref, gain), (router_ref, router)):
        values = small[...].astype(F32)
        for t in range(NX):
            wide[t] = jnp.concatenate([values[t * 8 + i : t * 8 + i + 1] for i in range(8)], axis=1)

    sib = me.at(c=1 - c)
    barrier = pltpu.get_barrier_semaphore()
    neighbours = [
        me.at(x=(x + 1) % NX),
        me.at(x=(x + 3) % NX),
        me.at(y=(y + 1) % NY),
        me.at(y=(y + 3) % NY),
        me.at(z=(z + 1) % NZ),
        me.at(z=(z + 7) % NZ),
        sib,
    ]
    for device in neighbours:
        pl.semaphore_signal(barrier, 1, device_id=device, device_id_type=MESH)

    @pl.when(x != y)
    def _():
        for h in range(2):
            pl.semaphore_signal(
                barrier, 1, device_id=me.at(x=y, y=x, c=h), device_id_type=MESH
            )

    here = lax.broadcasted_iota(jnp.int32, (64, 128), 1)
    there = lax.broadcasted_iota(jnp.int32, (64, 128), 0)
    spread = jnp.where(here == there + 64 * c, 1.0, 0.0).astype(BF16)
    for h in range(2):
        wsend[h] = dot_t0(wo_ref[:, h * 256 : (h + 1) * 256], spread).astype(BF16)

    own = me.s

    def look(j, carry):
        rank, hit, first, second = carry
        seg = seg_ref[j]
        same = seg == own
        return (
            rank + jnp.where(seg < own, 1, 0),
            jnp.where(same, 1, hit),
            jnp.where(same, blk_ref[0, j], first),
            jnp.where(same, blk_ref[1, j], second),
        )

    zero = jnp.int32(0)
    rank, filled, first, second = lax.fori_loop(0, SEGS, look, (zero, zero, zero, zero))

    tok_copy.wait()
    for s, block in enumerate((first, second)):
        xg[s][0] = tok[block]

    @pl.when(x != y)
    def _():
        pl.semaphore_wait(barrier, 9)

    @pl.when(x == y)
    def _():
        pl.semaphore_wait(barrier, 7)

    xcp = Copies(x_ss, x_rs)
    x0 = ring_x(me, xg0, xcp, 0)
    x1 = ring_x(me, xg1, xcp, 4)
    run(x0, 1)
    run(x1, 1)

    def w_copy(h, slot, device):
        return pltpu.make_async_remote_copy(
            src_ref=wsend.at[h],
            dst_ref=wrecv.at[slot],
            send_sem=w_ss.at[h],
            recv_sem=w_rs.at[slot],
            device_id=device,
            device_id_type=MESH,
        )

    @pl.when(x != y)
    def _():
        for h in range(2):
            w_copy(h, c, me.at(x=y, y=x, c=h)).start()

    @pl.when(x == y)
    def _():
        w_copy(1 - c, c, sib).start()
        wrecv[c] = wsend[c]

    wk_copy.wait()
    wv_copy.wait()
    wkv[:, :, 0:HD] = wk[...]
    wkv[:, :, HD : 2 * HD] = wv[...]

    @pl.when(x != y)
    def _():
        for h in range(2):
            w_copy(h, h, me.at(x=y, y=x, c=h)).wait()

    @pl.when(x == y)
    def _():
        w_copy(1 - c, 1 - c, sib).wait()

    wg[0, 0, 0] = wrecv[0] + wrecv[1]
    gw = gather_yz(me, wg, Copies(gw_ss, gw_rs))
    run(gw, 3)

    run(x0, 1)
    run(x1, 1)
    run(gw, 1)

    feat = [(x + d) % NX for d in range(NX)]

    def norm(s):
        rows = slice(s * BLK, (s + 1) * BLK)
        squares = jnp.zeros((BLK, 1), F32)
        routed = jnp.zeros((BLK, 1), F32)
        for d in range(NX):
            part = xg[s][d].astype(F32)
            squares += jnp.sum(part * part, axis=1, keepdims=True)
            routed += jnp.sum(part * router[feat[d]], axis=1, keepdims=True)
        scale = lax.rsqrt(squares * (1.0 / (NX * FEATS)) + 1e-05)
        gates[rows] = jax.nn.sigmoid(routed)
        for d in range(NX):
            normed[s][d] = (xg[s][d].astype(F32) * scale * gain[feat[d]]).astype(BF16)

    def through(s, weight):
        total = dot(normed[s][0], weight[feat[0]])
        for d in range(1, NX):
            total += dot(normed[s][d], weight[feat[d]])
        return total.astype(BF16)

    def keys(s, kv):
        found = through(s, wkv)
        kv[0, 0, 0] = jnp.concatenate(
            [found[:, 0:HD], found[:, HD : 2 * HD].astype(F32).T.astype(BF16)], axis=0
        )

    def queries(s):
        found = through(s, wq).astype(F32) * Q_SCALE
        for h in range(LOCAL_HEADS):
            columns = slice(s * QROWS + h * BLK, s * QROWS + (h + 1) * BLK)
            turned = found[:, h * HD : (h + 1) * HD].T
            high = turned.astype(BF16)
            qt[0:HD, columns] = high
            qt[HD : 2 * HD, columns] = (turned - high.astype(F32)).astype(BF16)

    ones = jnp.ones((BLK, HD), BF16)

    def twice(key):
        return jnp.concatenate([key, key], axis=1)

    def weigh(scores, most, value_t):
        return dot(value_t, jnp.exp(scores - most).astype(BF16))

    def with_sum(value, mark):
        return jnp.concatenate([value, mark], axis=0)

    def own_blocks():
        own0, own1 = kv0[0, 0, 0], kv1[0, 0, 0]
        key0, value0 = own0[0:BLK], with_sum(own0[BLK : 2 * BLK], ones)
        key1, value1 = own1[0:BLK], with_sum(own1[BLK : 2 * BLK], ones)
        key = lax.broadcasted_iota(jnp.int32, (BLK, QROWS), 0)
        query = lax.broadcasted_iota(jnp.int32, (BLK, QROWS), 1) % BLK
        seen = key <= query
        columns = slice(0, QROWS)
        s00 = jnp.where(seen, dot(twice(key0), qt[:, columns]), MASKED)
        most = jnp.max(s00, axis=0, keepdims=True)
        top[:, columns] = most
        acc[:, columns] = weigh(s00, most, value0)[0:ACC]
        columns = slice(QROWS, 2 * QROWS)
        s10 = dot(twice(key0), qt[:, columns])
        s11 = jnp.where(seen, dot(twice(key1), qt[:, columns]), MASKED)
        most = jnp.max(jnp.maximum(s10, s11), axis=0, keepdims=True)
        top[:, columns] = most
        acc[:, columns] = (weigh(s10, most, value0) + weigh(s11, most, value1))[0:ACC]

    nothing = jnp.zeros((BLK, HD), BF16)

    def attend(kv, chunk, stand_in):
        key_parts, value_parts, marks = [], [], []
        for i in range(KEY_SEGS):
            j = chunk * KEY_SEGS + i
            home = seg_ref[j]
            block = kv[(home + c) & 1, ((home >> 4) + NY - y) & 3, ((home >> 1) + NZ - z) & 7]
            seen = j < rank
            key_parts.append(jnp.where(seen, block[0:BLK], stand_in))
            value_parts.append(jnp.where(seen, block[BLK : 2 * BLK], nothing))
            marks.append(jnp.where(seen, ones, nothing))
        key_chunk = twice(jnp.concatenate(key_parts, axis=0))
        value_t = with_sum(
            jnp.concatenate(value_parts, axis=1), jnp.concatenate(marks, axis=1)
        )
        tile = 256
        for t in range(2 * QROWS // tile):
            columns = slice(t * tile, (t + 1) * tile)
            scores = dot(key_chunk, qt[:, columns])
            old = top[:, columns]
            new = jnp.maximum(old, jnp.max(scores, axis=0, keepdims=True))
            top[:, columns] = new
            acc[:, columns] = (
                acc[:, columns] * jnp.exp(old - new) + weigh(scores, new, value_t)[0:ACC]
            )

    def attend_some(kv, low, high):
        stand_in = jnp.broadcast_to(kv0[0, 0, 0][0:1], (BLK, HD))

        def step(chunk, carry):
            attend(kv, chunk, stand_in)
            return carry

        lax.fori_loop(low, high, step, 0)

    chunks = SEGS // KEY_SEGS

    run(x0)
    norm(0)
    keys(0, kv0)
    g0 = gather_yz(me, kv0, Copies(g0_ss, g0_rs))
    run(g0, 1)
    wq_copy.wait()
    queries(0)
    run(x1)
    norm(1)
    keys(1, kv1)
    g1 = gather_yz(me, kv1, Copies(g1_ss, g1_rs))
    run(g1, 1)
    run(g0, 2)
    run(gw, 3)
    run(g1, 2)
    run(g0, 1)
    run(gw, 1)
    queries(1)
    run(g0, 1)
    run(g1, 1)
    run(gw, 1)
    run(g0, 1)
    run(gw, 1)
    for _ in range(4):
        run(g0, 1)
        run(g1, 1)
        run(gw, 1)
    own_blocks()
    run(g0)
    for low in range(chunks):
        attend_some(kv0, low, low + 1)
        run(g1, 2)
    run(g1)
    run(gw)
    attend_some(kv1, 0, chunks)

    h0 = ring_x(me, hg0, xcp, 8)
    h1 = ring_x(me, hg1, xcp, 12)

    def finish(s):
        parts = []
        for h in range(LOCAL_HEADS):
            columns = slice(s * QROWS + h * BLK, s * QROWS + (h + 1) * BLK)
            parts.append((acc[0:HD, columns] / acc[HD : HD + 1, columns]).T.astype(BF16))
        hg[s][0] = jnp.concatenate(parts, axis=1)

    finish(0)
    run(h0, 1)
    finish(1)
    run(h1, 1)

    def project(d, begin):
        heads = jnp.concatenate([hg0[d], hg1[d]], axis=0)
        dy = (x + d + NY - y) % NY
        for j in range(NZ // 2):
            weight = jnp.concatenate(
                [
                    jnp.concatenate(
                        [wg[(k + c) % 2, dy, (2 * j + i + NZ - z) % NZ] for i in range(2)], axis=1
                    )
                    for k in range(2)
                ],
                axis=0,
            )
            lanes = slice(j * 256, (j + 1) * 256)
            term = dot(heads, weight)
            att[:, lanes] = term if begin else att[:, lanes] + term

    project(0, True)
    run(h0, 1)
    run(h1, 1)
    project(3, False)
    project(1, False)
    run(h0)
    run(h1)
    project(2, False)
    own_rows = jnp.concatenate([xg0[0], xg1[0]], axis=0)
    new_rows = own_rows.astype(F32) + gates[...] * att[...]
    out_ref[...] = jnp.where(filled == 1, new_rows, 0.0).astype(BF16)
    xcp.drain()


def on_device(tokens, norm_gain, router_weight, w_query, w_key, w_value, w_out, seg_ids, blk_ids):
    any_space = pl.BlockSpec(memory_space=pl.ANY)
    vmem = pl.BlockSpec(memory_space=pltpu.VMEM)
    smem = pl.BlockSpec(memory_space=pltpu.SMEM)
    dma = pltpu.SemaphoreType.DMA
    new_rows = pl.pallas_call(
        kernel,
        out_shape=jax.ShapeDtypeStruct((ROWS, FEATS), BF16),
        in_specs=[smem, smem, vmem, vmem, any_space, any_space, any_space, any_space, vmem],
        out_specs=vmem,
        scratch_shapes=[
            pltpu.VMEM((16, BLK, FEATS), BF16),
            pltpu.VMEM((NX, FEATS, 512), BF16),
            pltpu.VMEM((NX, FEATS, HD), BF16),
            pltpu.VMEM((NX, FEATS, HD), BF16),
            pltpu.VMEM((NX, FEATS, 2 * HD), BF16),
            pltpu.VMEM((NX, 1, FEATS), F32),
            pltpu.VMEM((NX, 1, FEATS), F32),
            pltpu.VMEM((NX, BLK, FEATS), BF16),
            pltpu.VMEM((NX, BLK, FEATS), BF16),
            pltpu.VMEM((NX, BLK, FEATS), BF16),
            pltpu.VMEM((NX, BLK, FEATS), BF16),
            pltpu.VMEM((2, 256, 128), BF16),
            pltpu.VMEM((2, 256, 128), BF16),
            pltpu.VMEM((2, NY, NZ, 256, 128), BF16),
            pltpu.VMEM((2, NY, NZ, 256, 128), BF16),
            pltpu.VMEM((2, NY, NZ, 256, 128), BF16),
            pltpu.VMEM((2 * HD, 2 * QROWS), BF16),
            pltpu.VMEM((ACC, 2 * QROWS), F32),
            pltpu.VMEM((1, 2 * QROWS), F32),
            pltpu.VMEM((ROWS, 1), F32),
            pltpu.VMEM((NX, BLK, 512), BF16),
            pltpu.VMEM((NX, BLK, 512), BF16),
            pltpu.VMEM((ROWS, FEATS), F32),
            dma((4,)),
            dma((2,)),
            dma((2,)),
            dma((COPIES,)),
            dma((COPIES,)),
            dma((COPIES,)),
            dma((COPIES,)),
            dma((COPIES,)),
            dma((COPIES,)),
            dma((16,)),
            dma((16,)),
        ],
        compiler_params=pltpu.CompilerParams(
            collective_id=0, has_side_effects=True, vmem_limit_bytes=56 << 20
        ),
        name="depth_layer",
    )(
        seg_ids,
        blk_ids.T,
        norm_gain.reshape(NX * 8, HD),
        router_weight.reshape(NX * 8, HD),
        tokens.reshape(16, BLK, FEATS),
        w_query.reshape(NX, FEATS, 512),
        w_key.reshape(NX, FEATS, HD),
        w_value.reshape(NX, FEATS, HD),
        w_out.T,
    )
    return new_rows.reshape(2, BLK, FEATS)


def solution(mesh):
    placed = (
        P("seq", "tp"),
        P(),
        P(),
        P(None, "tp"),
        P(None, "tp"),
        P(None, "tp"),
        P("tp", "seq"),
        P(),
        P(),
    )
    return jax.shard_map(
        on_device, mesh=mesh, in_specs=placed, out_specs=P("seq", None, "tp"), check_vma=False
    )
```
